128 devices in a mesh: chan: 8 (over y, x_lo), blk: 16 (over x_hi, z, core).
Axes of the slice: x: 4 (x_hi: 2, x_lo: 2; x = x_hi * 2 + x_lo), y: 4, z: 4, core: 2. Of those that a mesh axis runs over, the one named last changes fastest.
Arguments:
- voltages: bfloat16 [2, 16, 64, 536576], P(None, 'blk', 'chan'), may hold values from -5.5 to 5.5
- fir_taps: float32 [4, 4096], replicated, may hold values from -3 to 3
- station_flags: int32 [512], replicated, may hold values 0 or 1
- bin_offsets: int32 [256], replicated, may hold values from 0 to 3
Outputs:
- visibilities: bfloat16 [256, 2, 1024, 1024], P('chan', None, 'blk')
The draws below stay inside these ranges and needn't reach their ends.
All inputs are finite; a program needn't handle non-finite values.
Results may differ from the reference program's by a relative error of at most 0.0034.
Values may be sent and summed in bfloat16 or wider, within the bound.
No kernel may reach another device: no remote copies, remote signals or barrier semaphores. Data moves between devices by JAX's collectives and lax.ppermute only.
A program may use at most 256 MiB of HBM per device.

```python
import math
import jax
import jax.numpy as jnp
from jax import lax

STATIONS = 512
INPUTS = 1024
NFFT = 4096
KEEP = 256
TAPS = 4
FRAMES = 128
SAMPLES = 536576
BLOCKS = 16
IN_BLK = 64


def draw_voltages(key, part):
    common_key, gain_key, noise_key = jax.random.split(key, 3)
    shape = (2, BLOCKS, IN_BLK, SAMPLES)
    common = jax.random.normal(common_key, (2, 1, 1, SAMPLES), jnp.float32)
    noise = jax.random.normal(noise_key, shape, jnp.float32)
    gains = jnp.exp(jax.random.uniform(gain_key, (1, BLOCKS, IN_BLK, 1), jnp.float32, math.log(0.3), math.log(1.5)))
    values = jnp.clip(0.8 * gains * common + noise, -5.5, 5.5)
    return values.astype(jnp.bfloat16)


def touch_ends(result, rng, smallest, high):
    longest = result.shape.index(max(result.shape))
    spots = []
    for shift in (0, 1):
        where = [jax.random.randint(jax.random.fold_in(rng, axis), (), 0, length) for axis, length in enumerate(result.shape)]
        where[longest] = (where[longest] + shift) % result.shape[longest]
        spots.append(tuple(where))
    return result.at[spots[0]].set(smallest).at[spots[1]].set(high)


def normal_values(key, shape, spread, bound, kind=jnp.bfloat16):
    return jnp.clip(spread * jax.random.normal(key, shape, jnp.float32), -bound, bound).astype(kind)


def setup_inputs(seed: int = 0) -> dict:
    splits = jax.random.split(jax.random.key(seed), 5)
    return {
        "voltages": draw_voltages(jax.random.fold_in(splits[4], 71), 0),
        "fir_taps": normal_values(splits[1], (TAPS, NFFT), TAPS ** -0.5, 3.0, jnp.float32),
        "station_flags": touch_ends((jax.random.randint(splits[2], (STATIONS,), 0, 8) < 7).astype(jnp.int32), jax.random.fold_in(splits[2], 1), 0, 1),
        "bin_offsets": touch_ends(jax.random.randint(splits[3], (KEEP,), 0, 4), jax.random.fold_in(splits[3], 1), 0, 3).astype(jnp.int32),
    }


def filter_frames(block, fir_taps):
    data = block.astype(jnp.float32)
    filtered = jnp.zeros(data.shape[:2] + (FRAMES, NFFT), jnp.float32)
    for tap_index in range(TAPS):
        filtered = filtered + data[:, :, tap_index:tap_index + FRAMES, :] * fir_taps[tap_index]
    return filtered

def reference(voltages, fir_taps, station_flags, bin_offsets):
    planes = voltages.reshape(2, INPUTS, FRAMES + TAPS - 1, NFFT)
    weights = jnp.repeat(station_flags, 2).astype(jnp.float32)
    stride = 8

    def channelise(group):
        first = (group * stride).astype(jnp.int32)
        block = lax.dynamic_slice_in_dim(planes, first, stride, 1)
        filtered = filter_frames(block, fir_taps)
        spectrum = jnp.fft.fft(filtered[0] + 1j * filtered[1], axis=-1)[..., :KEEP]
        factor = lax.dynamic_slice_in_dim(weights, first, stride, 0)[:, None, None]
        real_part = jnp.real(spectrum) / math.sqrt(2.0 * NFFT) * factor
        imag_part = jnp.imag(spectrum) / math.sqrt(2.0 * NFFT) * factor
        return jnp.stack([real_part, imag_part]).astype(jnp.bfloat16)
    grouped = lax.map(channelise, jnp.arange(INPUTS // stride, dtype=jnp.int32))
    spectra = grouped.transpose(1, 4, 0, 2, 3).reshape(2, KEEP, INPUTS, FRAMES)
    scales = jnp.exp2(-bin_offsets.astype(jnp.float32)) / FRAMES

    def correlate(channel):
        block = lax.dynamic_index_in_dim(spectra, channel, 1, keepdims=False).astype(jnp.float32)
        rotated = jnp.stack([-block[1], block[0]])
        real_part = jnp.einsum('pif,pjf->ij', block, block)
        imag_part = jnp.einsum('pif,pjf->ij', block, rotated)
        return (jnp.stack([real_part, imag_part]) * scales[channel]).astype(jnp.bfloat16)
    return lax.map(correlate, jnp.arange(KEEP, dtype=jnp.int32))
```

```python
import functools
import math

import jax
import jax.numpy as jnp
import ml_dtypes
import numpy as np
from jax import lax
from jax.experimental import pallas as pl
from jax.experimental.pallas import tpu as pltpu
from jax.sharding import PartitionSpec as P

NFFT = 4096
HALF = NFFT // 2
TAPS = 4
FRAMES = 128
CHUNK = 64
STEP = 32


def dft_tables():
    n = np.arange(HALF)[:, None]
    tables = []
    for cls in range(2):
        channel = 2 * np.arange(128)[None, :] + cls
        angle = 2.0 * np.pi * ((n * channel) % NFFT) / NFFT
        table = np.concatenate([np.cos(angle), np.sin(angle)], axis=1)
        high = table.astype(ml_dtypes.bfloat16)
        low = (table - high.astype(np.float64)).astype(ml_dtypes.bfloat16)
        tables.append(np.stack([high, low]))
    return np.stack(tables)


def spectra_kernel(first_frame, x_hbm, taps_ref, table_ref, weight_ref, out_ref, x_vmem, fold, sums, turned, sems):
    lanes = STEP * NFFT
    halo = (TAPS - 1) * NFFT
    copies = []
    for s in range(CHUNK // STEP):
        start = 0 if s == 0 else s * lanes + halo
        size = lanes + halo if s == 0 else lanes
        copies.append(
            pltpu.make_async_copy(
                x_hbm.at[:, 0, :, pl.ds(first_frame * NFFT + start, size)],
                x_vmem.at[:, :, pl.ds(start, size)],
                sems.at[s],
            )
        )
    for copy in copies:
        copy.start()
    rows = STEP * 8
    for s in range(CHUNK // STEP):
        copies[s].wait()

        def fir(t, carry):
            p = t // 16
            n0 = pl.multiple_of((t % 16) * 128, 128)

            def load(f, offset):
                lane = pl.multiple_of((s * STEP + f) * NFFT + offset + n0, 128)
                return x_vmem[p, :, pl.ds(lane, 128)].astype(jnp.float32)

            def tap(k, offset):
                return jnp.broadcast_to(taps_ref[k : k + 1, pl.ds(n0 + offset, 128)], (8, 128))

            taps = [[tap(k, offset) for k in range(TAPS)] for offset in (0, HALF)]
            window = [[load(f, offset) for f in range(TAPS - 1)] for offset in (0, HALF)]
            for pair in range(STEP // 2):
                even, odd = [], []
                for f in (2 * pair, 2 * pair + 1):
                    halves = []
                    for w, h, offset in zip(window, taps, (0, HALF)):
                        w.append(load(f + TAPS - 1, offset))
                        halves.append(((w[0] * h[0] + w[1] * h[1]) + w[2] * h[2]) + w[3] * h[3])
                        w.pop(0)
                    even.append(halves[0] + halves[1])
                    odd.append(halves[0] - halves[1])
                where = pl.ds(pl.multiple_of(p * rows, rows) + pair * 16, 16)
                for cls, both in enumerate((even, odd)):
                    value = jnp.concatenate(both, axis=0)
                    high = value.astype(jnp.bfloat16)
                    low = (value - high.astype(jnp.float32)).astype(jnp.bfloat16)
                    fold[cls, 0, where, pl.ds(n0, 128)] = high
                    fold[cls, 1, where, pl.ds(n0, 128)] = low
            return carry

        lax.fori_loop(0, 32, fir, 0)
        for cls in range(2):
            total = jnp.dot(fold[cls, 0], table_ref[cls, 0], preferred_element_type=jnp.float32)
            total += jnp.dot(fold[cls, 1], table_ref[cls, 0], preferred_element_type=jnp.float32)
            total += jnp.dot(fold[cls, 0], table_ref[cls, 1], preferred_element_type=jnp.float32)
            real = total[:rows, :128] + total[rows:, 128:]
            imag = total[rows:, :128] - total[:rows, 128:]
            weight = weight_ref[...]
            real = (real.reshape(STEP, 8, 128) * weight).reshape(rows, 128)
            imag = (imag.reshape(STEP, 8, 128) * weight).reshape(rows, 128)
            sums[cls, s * rows : (s + 1) * rows, :] = real
            sums[cls, CHUNK * 8 + s * rows : CHUNK * 8 + (s + 1) * rows, :] = imag
    for cls in range(2):
        for i in range(8):
            turned[cls, i * 128 : (i + 1) * 128, :] = sums[cls, pl.ds(i, 128, stride=8), :].T

    def emit(g, carry):
        for cls in range(2):
            for j in range(16):
                out_ref[g, cls, j] = turned[cls, pl.ds(g * 16 + j, 8, stride=128), :].astype(jnp.bfloat16)
        return carry

    lax.fori_loop(0, 8, emit, 0)


def spectra(first_frame, x, taps, tables, weight):
    return pl.pallas_call(
        functools.partial(spectra_kernel, first_frame),
        out_shape=jax.ShapeDtypeStruct((8, 2, 16, 8, 128), jnp.bfloat16),
        in_specs=[pl.BlockSpec(memory_space=pl.ANY)] + [pl.BlockSpec(memory_space=pltpu.VMEM)] * 3,
        out_specs=pl.BlockSpec(memory_space=pltpu.VMEM),
        scratch_shapes=[
            pltpu.VMEM((2, 8, (CHUNK + TAPS - 1) * NFFT), jnp.bfloat16),
            pltpu.VMEM((2, 2, 2 * STEP * 8, HALF), jnp.bfloat16),
            pltpu.VMEM((2, 2 * CHUNK * 8, 128), jnp.float32),
            pltpu.VMEM((2, 8 * 128, 128), jnp.float32),
            pltpu.SemaphoreType.DMA((CHUNK // STEP,)),
        ],
        compiler_params=pltpu.CompilerParams(vmem_limit_bytes=56 * 1024 * 1024),
        cost_estimate=pl.CostEstimate(flops=6_500_000_000, bytes_accessed=14_000_000, transcendentals=0),
        name="spectra",
    )(x, taps, tables, weight)


NJ = 2


def correlate_kernel(blk_ref, scale_ref, *refs):
    sources, (out_ref, held, sems) = refs[:32], refs[32:]
    step, steps = pl.program_id(0), pl.num_programs(0)
    blk = blk_ref[0]

    def copies(at):
        slot = at % 2
        made = []
        for m in range(16):
            row = pl.multiple_of((blk ^ m) * 64, 64)
            for part in range(2):
                made.append(
                    pltpu.make_async_copy(
                        sources[2 * m + part].at[:, pl.ds(at * NJ, NJ)],
                        held.at[slot, :, :, pl.ds(row, 64), pl.ds(part * 128, 128)],
                        sems.at[slot, 2 * m + part],
                    )
                )
        return made

    @pl.when(step == 0)
    def _():
        for copy in copies(step):
            copy.start()

    @pl.when(step + 1 < steps)
    def _():
        for copy in copies(step + 1):
            copy.start()

    for copy in copies(step):
        copy.wait()
    slot = step % 2
    own = pl.ds(pl.multiple_of(blk * 64, 64), 64)
    lane = lax.broadcasted_iota(jnp.int32, (64, 128), 1)
    sign = jnp.where(lane < 64, 1.0, -1.0)
    for cls in range(2):
        for jj in range(NJ):
            mine = held[slot, cls, jj, own, :]
            wide = mine.astype(jnp.float32)
            turned = [pltpu.roll(wide[:, h : h + 128], 64, 1) * sign for h in (0, 128)]
            left = jnp.concatenate([mine, jnp.concatenate(turned, axis=1).astype(jnp.bfloat16)], axis=0)
            total = lax.dot_general(
                left, held[slot, cls, jj], (((1,), (1,)), ((), ())), preferred_element_type=jnp.float32
            )
            channel = 2 * jj + cls
            total = (total * scale_ref[step * (2 * NJ) + channel]).astype(jnp.bfloat16)
            out_ref[channel, 0] = total[:64]
            out_ref[channel, 1] = total[64:]


def correlate(blk, scale, sources):
    return pl.pallas_call(
        correlate_kernel,
        out_shape=jax.ShapeDtypeStruct((32, 2, 64, 1024), jnp.bfloat16),
        grid=(16 // NJ,),
        in_specs=[pl.BlockSpec(memory_space=pltpu.SMEM)] * 2 + [pl.BlockSpec(memory_space=pltpu.HBM)] * 32,
        out_specs=pl.BlockSpec((2 * NJ, 2, 64, 1024), lambda s: (s, 0, 0, 0)),
        scratch_shapes=[
            pltpu.VMEM((2, 2, NJ, 1024, 256), jnp.bfloat16),
            pltpu.SemaphoreType.DMA((2, 32)),
        ],
        compiler_params=pltpu.CompilerParams(vmem_limit_bytes=56 * 1024 * 1024),
        cost_estimate=pl.CostEstimate(flops=2_200_000_000, bytes_accessed=25_000_000, transcendentals=0),
        name="correlate",
    )(blk, scale, *sources)


def send(array, bits):
    return lax.ppermute(array, "blk", [(b, b ^ bits) for b in range(16)])


X2, Z1, Z3, CORE = 8, 2, 6, 1


def turn(chunk):
    got = lax.all_to_all(chunk, "chan", split_axis=0, concat_axis=0, tiled=True)
    return got.transpose(1, 2, 0, 3, 4).reshape(2, 16, 64, 128)


def on_device(voltages, fir_taps, station_flags, bin_offsets):
    chan, blk = lax.axis_index("chan"), lax.axis_index("blk")
    flags = jnp.repeat(station_flags, 2).astype(jnp.float32)
    weight = lax.dynamic_slice_in_dim(flags, blk * 64 + chan * 8, 8, 0) / math.sqrt(2.0 * NFFT)
    weight = jnp.broadcast_to(weight[:, None], (8, 128))
    scales = jnp.exp2(-bin_offsets.astype(jnp.float32)) / FRAMES
    scale = lax.dynamic_slice_in_dim(scales, chan * 32, 32, 0)
    tables = jnp.asarray(dft_tables())

    first = turn(spectra(0, voltages, fir_taps, tables, weight))
    second = turn(spectra(CHUNK, voltages, fir_taps, tables, weight))
    one = {0: first}
    one[Z1] = send(first, Z1)
    one[Z3] = send(first, Z3)
    one[X2] = send(first, X2)
    one[Z1 ^ Z3] = send(one[Z3], Z1)
    one[X2 ^ Z1] = send(one[Z1], X2)
    one[X2 ^ Z3] = send(one[Z3], X2)
    one[X2 ^ Z1 ^ Z3] = send(one[Z1 ^ Z3], X2)
    two = {0: second}
    two[X2] = send(second, X2)
    for m in (0, X2):
        two[m ^ Z1] = send(two[m], Z1)
        two[m ^ Z3] = send(two[m], Z3)
    two[Z1 ^ Z3] = send(two[Z1], Z3)
    two[X2 ^ Z1 ^ Z3] = send(two[X2 ^ Z3], Z1)
    for part in (one, two):
        for m in list(part):
            part[m ^ CORE] = send(part[m], CORE)
    sources = []
    for m in range(16):
        sources += [one[m], two[m]]
    return correlate(blk.astype(jnp.int32).reshape(1), scale, sources)


def solution(mesh):
    in_specs = (P(None, "blk", "chan", None), P(), P(), P())
    out_specs = P("chan", None, "blk", None)
    return jax.shard_map(
        on_device, mesh=mesh, in_specs=in_specs, out_specs=out_specs, check_vma=False
    )
```

```python
import functools
import math

import jax
import jax.numpy as jnp
import ml_dtypes
import numpy as np
from jax import lax
from jax.experimental import pallas as pl
from jax.experimental.pallas import tpu as pltpu
from jax.sharding import PartitionSpec as P

NFFT = 4096
HALF = NFFT // 2
TAPS = 4
FRAMES = 128
CHUNK = 64


def dft_tables():
    n = np.arange(HALF)[:, None]
    tables = []
    for cls in range(2):
        channel = 2 * np.arange(128)[None, :] + cls
        angle = 2.0 * np.pi * ((n * channel) % NFFT) / NFFT
        table = np.concatenate([np.cos(angle), np.sin(angle)], axis=1)
        high = table.astype(ml_dtypes.bfloat16)
        low = (table - high.astype(np.float64)).astype(ml_dtypes.bfloat16)
        tables.append(np.stack([high, low]))
    return np.stack(tables)


BLOCK = 256
BLOCKS = HALF // BLOCK


def spectra_kernel(
    first_frame, x_hbm, taps_ref, table_hbm, weight_ref, out_ref,
    x_vmem, table, fold_a, fold_b, total, sums, turned, x_sems, table_sems,
):
    frames = CHUNK + TAPS - 1
    rows = CHUNK * 8
    x_copies, table_copies = [], []
    for kb in range(BLOCKS):
        for half in range(2):
            lanes = pl.ds(half * HALF + kb * BLOCK, BLOCK)
            x_copies.append(
                pltpu.make_async_copy(
                    x_hbm.at[:, pl.ds(first_frame, frames), :, lanes],
                    x_vmem.at[:, :, :, lanes],
                    x_sems.at[kb, half],
                )
            )
        samples = pl.ds(kb * BLOCK, BLOCK)
        table_copies.append(
            pltpu.make_async_copy(table_hbm.at[:, :, samples], table.at[:, :, samples], table_sems.at[kb])
        )
    for kb in range(BLOCKS):
        x_copies[2 * kb].start()
        x_copies[2 * kb + 1].start()
        table_copies[kb].start()

    def fir(kb, p, tile, fold):
        n0 = pl.multiple_of(kb * BLOCK + tile * 128, 128)
        to = pl.ds(pl.multiple_of(tile * 128, 128), 128)

        def load(f, offset):
            return x_vmem[p, f, :, pl.ds(n0 + offset, 128)].astype(jnp.float32)

        def tap(k, offset):
            return jnp.broadcast_to(taps_ref[k : k + 1, pl.ds(n0 + offset, 128)], (8, 128))

        taps = [[tap(k, offset) for k in range(TAPS)] for offset in (0, HALF)]
        window = [[load(f, offset) for f in range(TAPS - 1)] for offset in (0, HALF)]
        for pair in range(CHUNK // 2):
            even, odd = [], []
            for f in (2 * pair, 2 * pair + 1):
                halves = []
                for w, h, offset in zip(window, taps, (0, HALF)):
                    w.append(load(f + TAPS - 1, offset))
                    halves.append(((w[0] * h[0] + w[1] * h[1]) + w[2] * h[2]) + w[3] * h[3])
                    w.pop(0)
                even.append(halves[0] + halves[1])
                odd.append(halves[0] - halves[1])
            for cls, both in enumerate((even, odd)):
                value = jnp.concatenate(both, axis=0)
                high = value.astype(jnp.bfloat16)
                low = (value - high.astype(jnp.float32)).astype(jnp.bfloat16)
                fold[p, cls, 0, pair * 16 : pair * 16 + 16, to] = high
                fold[p, cls, 1, pair * 16 : pair * 16 + 16, to] = low

    def product(kb, cls, p, fold):
        samples = pl.ds(pl.multiple_of(kb * BLOCK, BLOCK), BLOCK)
        high, low = fold[p, cls, 0], fold[p, cls, 1]
        left = jnp.concatenate([high, low, high], axis=1)
        table_high, table_low = table[cls, 0, samples, :], table[cls, 1, samples, :]
        right = jnp.concatenate([table_high, table_high, table_low], axis=0)
        return jnp.dot(left, right, preferred_element_type=jnp.float32)

    def stage(kb, fold_in, fold_out, first=False):
        def unit(u, carry):
            a, b = u // 2, u % 2
            if fold_out is not None:
                fir(kb + 1, a, b, fold_out)
            if fold_in is not None:
                value = product(kb, a, b, fold_in)
                if first:
                    total[a, b] = value
                else:
                    total[a, b] += value
            return carry

        lax.fori_loop(0, 4, unit, 0)

    def arrive(kb):
        x_copies[2 * kb].wait()
        x_copies[2 * kb + 1].wait()
        table_copies[kb].wait()

    arrive(0)
    stage(-1, None, fold_a)
    arrive(1)
    stage(0, fold_a, fold_b, first=True)
    arrive(2)
    stage(1, fold_b, fold_a)
    for kb in range(3, BLOCKS):
        arrive(kb)

    def two_stages(k, carry):
        stage(2 * k, fold_a, fold_b)
        stage(2 * k + 1, fold_b, fold_a)
        return carry

    lax.fori_loop(1, BLOCKS // 2 - 1, two_stages, 0)
    stage(BLOCKS - 2, fold_a, fold_b)
    stage(BLOCKS - 1, fold_b, None)
    weight = weight_ref[...]
    for cls in range(2):
        real = total[cls, 0, :, :128] + total[cls, 1, :, 128:]
        imag = total[cls, 1, :, :128] - total[cls, 0, :, 128:]
        sums[cls, :rows, :] = (real.reshape(CHUNK, 8, 128) * weight).reshape(rows, 128)
        sums[cls, rows:, :] = (imag.reshape(CHUNK, 8, 128) * weight).reshape(rows, 128)
    for cls in range(2):
        for i in range(8):
            turned[cls, i * 128 : (i + 1) * 128, :] = sums[cls, pl.ds(i, 128, stride=8), :].T

    def emit(g, carry):
        for cls in range(2):
            for j in range(16):
                out_ref[g, cls, j] = turned[cls, pl.ds(g * 16 + j, 8, stride=128), :].astype(jnp.bfloat16)
        return carry

    lax.fori_loop(0, 8, emit, 0)


def spectra(first_frame, x, taps, tables, weight):
    return pl.pallas_call(
        functools.partial(spectra_kernel, first_frame),
        out_shape=jax.ShapeDtypeStruct((8, 2, 16, 8, 128), jnp.bfloat16),
        in_specs=[
            pl.BlockSpec(memory_space=pltpu.HBM),
            pl.BlockSpec(memory_space=pltpu.VMEM),
            pl.BlockSpec(memory_space=pltpu.HBM),
            pl.BlockSpec(memory_space=pltpu.VMEM),
        ],
        out_specs=pl.BlockSpec(memory_space=pltpu.VMEM),
        scratch_shapes=[
            pltpu.VMEM((2, CHUNK + TAPS - 1, 8, NFFT), jnp.bfloat16),
            pltpu.VMEM((2, 2, HALF, 256), jnp.bfloat16),
            pltpu.VMEM((2, 2, 2, CHUNK * 8, BLOCK), jnp.bfloat16),
            pltpu.VMEM((2, 2, 2, CHUNK * 8, BLOCK), jnp.bfloat16),
            pltpu.VMEM((2, 2, CHUNK * 8, 256), jnp.float32),
            pltpu.VMEM((2, 2 * CHUNK * 8, 128), jnp.float32),
            pltpu.VMEM((2, 8 * 128, 128), jnp.float32),
            pltpu.SemaphoreType.DMA((BLOCKS, 2)),
            pltpu.SemaphoreType.DMA((BLOCKS,)),
        ],
        compiler_params=pltpu.CompilerParams(vmem_limit_bytes=56 * 1024 * 1024),
        cost_estimate=pl.CostEstimate(flops=6_500_000_000, bytes_accessed=14_000_000, transcendentals=0),
        name="spectra",
    )(x, taps, tables, weight)


NJ = 2


def correlate_kernel(blk_ref, scale_ref, *refs):
    sources, (out_ref, held, sems) = refs[:32], refs[32:]
    step, steps = pl.program_id(0), pl.num_programs(0)
    blk = blk_ref[0]

    def copies(at):
        slot = at % 2
        made = []
        for m in range(16):
            row = pl.multiple_of((blk ^ m) * 64, 64)
            for part in range(2):
                made.append(
                    pltpu.make_async_copy(
                        sources[2 * m + part].at[:, pl.ds(at * NJ, NJ)],
                        held.at[slot, :, :, pl.ds(row, 64), pl.ds(part * 128, 128)],
                        sems.at[slot, 2 * m + part],
                    )
                )
        return made

    @pl.when(step == 0)
    def _():
        for copy in copies(step):
            copy.start()

    @pl.when(step + 1 < steps)
    def _():
        for copy in copies(step + 1):
            copy.start()

    for copy in copies(step):
        copy.wait()
    slot = step % 2
    own = pl.ds(pl.multiple_of(blk * 64, 64), 64)
    lane = lax.broadcasted_iota(jnp.int32, (64, 128), 1)
    sign = jnp.where(lane < 64, 1.0, -1.0)
    for cls in range(2):
        for jj in range(NJ):
            mine = held[slot, cls, jj, own, :]
            wide = mine.astype(jnp.float32)
            turned = [pltpu.roll(wide[:, h : h + 128], 64, 1) * sign for h in (0, 128)]
            left = jnp.concatenate([mine, jnp.concatenate(turned, axis=1).astype(jnp.bfloat16)], axis=0)
            total = lax.dot_general(
                left, held[slot, cls, jj], (((1,), (1,)), ((), ())), preferred_element_type=jnp.float32
            )
            channel = 2 * jj + cls
            total = (total * scale_ref[step * (2 * NJ) + channel]).astype(jnp.bfloat16)
            out_ref[channel, 0] = total[:64]
            out_ref[channel, 1] = total[64:]


def correlate(blk, scale, sources):
    return pl.pallas_call(
        correlate_kernel,
        out_shape=jax.ShapeDtypeStruct((32, 2, 64, 1024), jnp.bfloat16),
        grid=(16 // NJ,),
        in_specs=[pl.BlockSpec(memory_space=pltpu.SMEM)] * 2 + [pl.BlockSpec(memory_space=pltpu.HBM)] * 32,
        out_specs=pl.BlockSpec((2 * NJ, 2, 64, 1024), lambda s: (s, 0, 0, 0)),
        scratch_shapes=[
            pltpu.VMEM((2, 2, NJ, 1024, 256), jnp.bfloat16),
            pltpu.SemaphoreType.DMA((2, 32)),
        ],
        compiler_params=pltpu.CompilerParams(vmem_limit_bytes=56 * 1024 * 1024),
        cost_estimate=pl.CostEstimate(flops=2_200_000_000, bytes_accessed=25_000_000, transcendentals=0),
        name="correlate",
    )(blk, scale, *sources)


def send(array, bits):
    return lax.ppermute(array, "blk", [(b, b ^ bits) for b in range(16)])


X2, Z1, Z3, CORE = 8, 2, 6, 1


def turn(chunk):
    got = lax.all_to_all(chunk, "chan", split_axis=0, concat_axis=0, tiled=True)
    return got.transpose(1, 2, 0, 3, 4).reshape(2, 16, 64, 128)


def on_device(voltages, fir_taps, station_flags, bin_offsets):
    chan, blk = lax.axis_index("chan"), lax.axis_index("blk")
    flags = jnp.repeat(station_flags, 2).astype(jnp.float32)
    weight = lax.dynamic_slice_in_dim(flags, blk * 64 + chan * 8, 8, 0) / math.sqrt(2.0 * NFFT)
    weight = jnp.broadcast_to(weight[:, None], (8, 128))
    scales = jnp.exp2(-bin_offsets.astype(jnp.float32)) / FRAMES
    scale = lax.dynamic_slice_in_dim(scales, chan * 32, 32, 0)
    tables = jnp.asarray(dft_tables())

    planes = voltages.reshape(2, 8, FRAMES + TAPS - 1, NFFT).transpose(0, 2, 1, 3)

    first = turn(spectra(0, planes, fir_taps, tables, weight))
    weight, first = lax.optimization_barrier((weight, first))
    later = spectra(CHUNK, planes, fir_taps, tables, weight)
    one = {0: first}
    for bits in (Z1, Z3, X2):
        one[bits] = send(first, bits)
    later, one[Z1], one[Z3], one[X2] = lax.optimization_barrier((later, one[Z1], one[Z3], one[X2]))
    one[Z1 ^ Z3] = send(one[Z3], Z1)
    one[X2 ^ Z1] = send(one[Z1], X2)
    one[X2 ^ Z3] = send(one[Z3], X2)
    one[X2 ^ Z1 ^ Z3] = send(one[Z1 ^ Z3], X2)
    second = turn(later)
    two = {0: second}
    two[X2] = send(second, X2)
    for m in (0, X2):
        two[m ^ Z1] = send(two[m], Z1)
        two[m ^ Z3] = send(two[m], Z3)
    two[Z1 ^ Z3] = send(two[Z1], Z3)
    two[X2 ^ Z1 ^ Z3] = send(two[X2 ^ Z3], Z1)
    for part in (one, two):
        for m in list(part):
            part[m ^ CORE] = send(part[m], CORE)
    sources = []
    for m in range(16):
        sources += [one[m], two[m]]
    return correlate(blk.astype(jnp.int32).reshape(1), scale, sources)


def solution(mesh):
    in_specs = (P(None, "blk", "chan", None), P(), P(), P())
    out_specs = P("chan", None, "blk", None)
    return jax.shard_map(
        on_device, mesh=mesh, in_specs=in_specs, out_specs=out_specs, check_vma=False
    )
```

```python
import functools
import math

import jax
import jax.numpy as jnp
import ml_dtypes
import numpy as np
from jax import lax
from jax.experimental import pallas as pl
from jax.experimental.pallas import tpu as pltpu
from jax.sharding import PartitionSpec as P

NFFT = 4096
HALF = NFFT // 2
TAPS = 4
FRAMES = 128
CHUNK = 64


def dft_tables():
    n = np.arange(HALF)[:, None]
    tables = []
    for cls in range(2):
        channel = 2 * np.arange(128)[None, :] + cls
        angle = 2.0 * np.pi * ((n * channel) % NFFT) / NFFT
        table = np.concatenate([np.cos(angle), np.sin(angle)], axis=1)
        high = table.astype(ml_dtypes.bfloat16)
        low = (table - high.astype(np.float64)).astype(ml_dtypes.bfloat16)
        tables.append(np.stack([high, low]))
    return np.stack(tables)


BLOCK = 256
BLOCKS = HALF // BLOCK


def spectra_kernel(
    first_frame, x_hbm, taps_ref, table_hbm, weight_ref, out_ref,
    x_vmem, table, fold_a, fold_b, total, sums, turned, x_sems, table_sems,
):
    frames = CHUNK + TAPS - 1
    rows = CHUNK * 8
    x_copies, table_copies = [], []
    for kb in range(BLOCKS):
        for half in range(2):
            lanes = pl.ds(half * HALF + kb * BLOCK, BLOCK)
            x_copies.append(
                pltpu.make_async_copy(
                    x_hbm.at[:, pl.ds(first_frame, frames), :, lanes],
                    x_vmem.at[:, :, :, lanes],
                    x_sems.at[kb, half],
                )
            )
        samples = pl.ds(kb * BLOCK, BLOCK)
        table_copies.append(
            pltpu.make_async_copy(table_hbm.at[:, :, samples], table.at[:, :, samples], table_sems.at[kb])
        )

    def fetch(kb):
        x_copies[2 * kb].start()
        x_copies[2 * kb + 1].start()
        table_copies[kb].start()

    fetch(0)
    fetch(1)

    def fir(kb, p, tile, fold):
        n0 = pl.multiple_of(kb * BLOCK + tile * 128, 128)
        to = pl.ds(pl.multiple_of(tile * 128, 128), 128)

        def load(f, offset):
            return x_vmem[p, f, :, pl.ds(n0 + offset, 128)].astype(jnp.float32)

        def tap(k, offset):
            return jnp.broadcast_to(taps_ref[k : k + 1, pl.ds(n0 + offset, 128)], (8, 128))

        taps = [[tap(k, offset) for k in range(TAPS)] for offset in (0, HALF)]
        window = [[load(f, offset) for f in range(TAPS - 1)] for offset in (0, HALF)]
        for pair in range(CHUNK // 2):
            even, odd = [], []
            for f in (2 * pair, 2 * pair + 1):
                halves = []
                for w, h, offset in zip(window, taps, (0, HALF)):
                    w.append(load(f + TAPS - 1, offset))
                    halves.append(((w[0] * h[0] + w[1] * h[1]) + w[2] * h[2]) + w[3] * h[3])
                    w.pop(0)
                even.append(halves[0] + halves[1])
                odd.append(halves[0] - halves[1])
            for cls, both in enumerate((even, odd)):
                value = jnp.concatenate(both, axis=0)
                high = value.astype(jnp.bfloat16)
                low = (value - high.astype(jnp.float32)).astype(jnp.bfloat16)
                fold[p, cls, 0, pair * 16 : pair * 16 + 16, to] = high
                fold[p, cls, 1, pair * 16 : pair * 16 + 16, to] = low

    def product(kb, cls, p, fold):
        samples = pl.ds(pl.multiple_of(kb * BLOCK, BLOCK), BLOCK)
        high, low = fold[p, cls, 0], fold[p, cls, 1]
        left = jnp.concatenate([high, low, high], axis=1)
        table_high, table_low = table[cls, 0, samples, :], table[cls, 1, samples, :]
        right = jnp.concatenate([table_high, table_high, table_low], axis=0)
        return jnp.dot(left, right, preferred_element_type=jnp.float32)

    def stage(kb, fold_in, fold_out, first=False):
        def unit(a, carry):
            if fold_out is not None:
                fir(kb + 1, a, 0, fold_out)
                fir(kb + 1, a, 1, fold_out)
            for b in range(2):
                if fold_in is not None:
                    value = product(kb, a, b, fold_in)
                    if first:
                        total[a, b] = value
                    else:
                        total[a, b] += value
            return carry

        lax.fori_loop(0, 2, unit, 0)

    def arrive(kb):
        x_copies[2 * kb].wait()
        x_copies[2 * kb + 1].wait()
        table_copies[kb].wait()

    arrive(0)
    for kb in range(2, BLOCKS):
        fetch(kb)
    stage(-1, None, fold_a)
    arrive(1)
    stage(0, fold_a, fold_b, first=True)
    arrive(2)
    stage(1, fold_b, fold_a)
    for kb in range(3, BLOCKS):
        arrive(kb)

    def two_stages(k, carry):
        stage(2 * k, fold_a, fold_b)
        stage(2 * k + 1, fold_b, fold_a)
        return carry

    lax.fori_loop(1, BLOCKS // 2 - 1, two_stages, 0)
    stage(BLOCKS - 2, fold_a, fold_b)
    stage(BLOCKS - 1, fold_b, None)
    weight = weight_ref[...]
    for cls in range(2):
        real = total[cls, 0, :, :128] + total[cls, 1, :, 128:]
        imag = total[cls, 1, :, :128] - total[cls, 0, :, 128:]
        sums[cls, :rows, :] = (real.reshape(CHUNK, 8, 128) * weight).reshape(rows, 128)
        sums[cls, rows:, :] = (imag.reshape(CHUNK, 8, 128) * weight).reshape(rows, 128)
    for cls in range(2):
        for i in range(8):
            turned[cls, i * 128 : (i + 1) * 128, :] = sums[cls, pl.ds(i, 128, stride=8), :].T

    def emit(g, carry):
        for cls in range(2):
            for j in range(16):
                out_ref[g, cls, j] = turned[cls, pl.ds(g * 16 + j, 8, stride=128), :].astype(jnp.bfloat16)
        return carry

    lax.fori_loop(0, 8, emit, 0)


def spectra(first_frame, x, taps, tables, weight):
    return pl.pallas_call(
        functools.partial(spectra_kernel, first_frame),
        out_shape=jax.ShapeDtypeStruct((8, 2, 16, 8, 128), jnp.bfloat16),
        in_specs=[
            pl.BlockSpec(memory_space=pltpu.HBM),
            pl.BlockSpec(memory_space=pltpu.VMEM),
            pl.BlockSpec(memory_space=pltpu.HBM),
            pl.BlockSpec(memory_space=pltpu.VMEM),
        ],
        out_specs=pl.BlockSpec(memory_space=pltpu.VMEM),
        scratch_shapes=[
            pltpu.VMEM((2, CHUNK + TAPS - 1, 8, NFFT), jnp.bfloat16),
            pltpu.VMEM((2, 2, HALF, 256), jnp.bfloat16),
            pltpu.VMEM((2, 2, 2, CHUNK * 8, BLOCK), jnp.bfloat16),
            pltpu.VMEM((2, 2, 2, CHUNK * 8, BLOCK), jnp.bfloat16),
            pltpu.VMEM((2, 2, CHUNK * 8, 256), jnp.float32),
            pltpu.VMEM((2, 2 * CHUNK * 8, 128), jnp.float32),
            pltpu.VMEM((2, 8 * 128, 128), jnp.float32),
            pltpu.SemaphoreType.DMA((BLOCKS, 2)),
            pltpu.SemaphoreType.DMA((BLOCKS,)),
        ],
        compiler_params=pltpu.CompilerParams(vmem_limit_bytes=56 * 1024 * 1024),
        cost_estimate=pl.CostEstimate(flops=6_500_000_000, bytes_accessed=14_000_000, transcendentals=0),
        name="spectra",
    )(x, taps, tables, weight)


NJ = 2


STEPS_Z = (0, 1, 3, 2)


def correlate_kernel(far, places, place_ref, scale_ref, *refs):
    out_ref, token_ref, staged, sems = refs[-4:]
    step, steps = pl.program_id(0), pl.num_programs(0)
    slot = step % 2
    first_column = (place_ref[0] ^ far) * 512
    place_z = place_ref[1]
    at_core_0 = place_ref[2] == 0
    token_ref[...] = jnp.zeros_like(token_ref)

    def copy(at):
        column = pl.multiple_of(first_column, 512)
        return pltpu.make_async_copy(
            staged.at[at % 2],
            out_ref.at[pl.ds(at * (2 * NJ), 2 * NJ), :, :, pl.ds(column, 512)],
            sems.at[at % 2],
        )

    @pl.when(step >= 2)
    def _():
        copy(step - 2).wait()

    lane = lax.broadcasted_iota(jnp.int32, (64, 128), 1)
    sign = jnp.where(lane < 64, 1.0, -1.0)
    for cls in range(2):
        for jj in range(NJ):

            def load(place):
                ref, *lead = place
                return refs[ref][(*lead, cls, jj)]

            own = [load(place) for place in places[:2]]
            turned = [(pltpu.roll(o.astype(jnp.float32), 64, 1) * sign).astype(jnp.bfloat16) for o in own]
            left = jnp.concatenate([jnp.concatenate(own, axis=1), jnp.concatenate(turned, axis=1)], axis=0)
            channel = 2 * jj + cls
            scale = scale_ref[step * (2 * NJ) + channel]
            for half in range(2):
                rows = []
                for k in (2 * half, 2 * half + 1):
                    same_p, other_p, same_q, other_q = [load(place) for place in places[2 + 4 * k : 6 + 4 * k]]
                    same = jnp.concatenate([same_p, same_q], axis=1)
                    other = jnp.concatenate([other_p, other_q], axis=1)
                    rows += [jnp.where(at_core_0, same, other), jnp.where(at_core_0, other, same)]
                right = jnp.concatenate(rows, axis=0)
                total = lax.dot_general(
                    left, right, (((1,), (1,)), ((), ())), preferred_element_type=jnp.float32
                )
                total = (total * scale).astype(jnp.bfloat16)
                for k in (2 * half, 2 * half + 1):
                    to = pl.ds(pl.multiple_of((place_z ^ STEPS_Z[k]) * 128, 128), 128)
                    lanes = slice(128 * (k % 2), 128 * (k % 2) + 128)
                    for plane in range(2):
                        staged[slot, channel, plane, :, to] = total[64 * plane : 64 * plane + 64, lanes]
    copy(step).start()

    @pl.when(step == steps - 1)
    def _():
        for at in (steps - 2, steps - 1):
            copy(at).wait()


def block_index(lead, step):
    return (0,) * lead + (step, 0, 0)


def correlate(far, place, scale, parts, token, out=None):
    operands, places = [], []
    for part in parts:
        array, *lead = part if isinstance(part, tuple) else (part,)
        known = [at for at, operand in enumerate(operands) if operand is array]
        if not known:
            operands.append(array)
        places.append((known[0] if known else len(operands) - 1, *lead))
    specs = [pl.BlockSpec(memory_space=pltpu.SMEM)] * 2
    for block in operands:
        lead = block.shape[:-4]
        specs.append(pl.BlockSpec((*lead, 2, NJ, 64, 128), functools.partial(block_index, len(lead) + 1)))
    specs.append(pl.BlockSpec(memory_space=pltpu.HBM))
    operands.append(token)
    aliases = {}
    if out is not None:
        specs.append(pl.BlockSpec(memory_space=pltpu.HBM))
        aliases = {2 + len(operands): 0}
        operands.append(out)
    return pl.pallas_call(
        functools.partial(correlate_kernel, far, places),
        out_shape=(
            jax.ShapeDtypeStruct((32, 2, 64, 1024), jnp.bfloat16),
            jax.ShapeDtypeStruct((8, 128), jnp.float32),
        ),
        grid=(16 // NJ,),
        in_specs=specs,
        out_specs=(pl.BlockSpec(memory_space=pltpu.HBM), pl.BlockSpec((8, 128), lambda s: (0, 0))),
        input_output_aliases=aliases,
        scratch_shapes=[
            pltpu.VMEM((2, 2 * NJ, 2, 64, 512), jnp.bfloat16),
            pltpu.SemaphoreType.DMA((2,)),
        ],
        compiler_params=pltpu.CompilerParams(vmem_limit_bytes=56 * 1024 * 1024),
        cost_estimate=pl.CostEstimate(flops=2_000_000_000, bytes_accessed=13_000_000, transcendentals=0),
        name="correlate",
    )(place, scale, *operands)


class Block:
    def __init__(self, value):
        self.value = value


def together(*blocks):
    values = lax.optimization_barrier(tuple(block.value for block in blocks))
    for block, value in zip(blocks, values):
        block.value = value


def along_x(block):
    return Block(lax.ppermute(block.value, "x_hi", [(0, 1), (1, 0)]))


def along_z(block, bits):
    return Block(lax.ppermute(block.value, "z", [(z, z ^ bits) for z in range(4)]))


def to_core(*blocks):
    return lax.ppermute(jnp.stack([block.value for block in blocks]), "core", [(0, 1), (1, 0)])


def turn(chunk):
    got = lax.all_to_all(chunk, ("y", "x_lo"), split_axis=0, concat_axis=0, tiled=True)
    return got.transpose(1, 2, 0, 3, 4).reshape(2, 16, 64, 128)


def on_device(voltages, fir_taps, station_flags, bin_offsets):
    chan = lax.axis_index(("y", "x_lo"))
    x_hi, z, core = [lax.axis_index(axis) for axis in ("x_hi", "z", "core")]
    blk = (x_hi * 4 + z) * 2 + core
    flags = jnp.repeat(station_flags, 2).astype(jnp.float32)
    weight = lax.dynamic_slice_in_dim(flags, blk * 64 + chan * 8, 8, 0) / math.sqrt(2.0 * NFFT)
    weight = jnp.broadcast_to(weight[:, None], (8, 128))
    scales = jnp.exp2(-bin_offsets.astype(jnp.float32)) / FRAMES
    scale = lax.dynamic_slice_in_dim(scales, chan * 32, 32, 0)
    tables = jnp.asarray(dft_tables())
    planes = voltages.reshape(2, 8, FRAMES + TAPS - 1, NFFT).transpose(0, 2, 1, 3)

    place = jnp.stack([x_hi, z, core]).astype(jnp.int32)
    p = {0: Block(turn(spectra(0, planes, fir_taps, tables, weight)))}
    weight = Block(weight)
    together(weight, p[0])
    spectra_q = Block(spectra(CHUNK, planes, fir_taps, tables, weight.value))
    xp, q, xq = {0: along_x(p[0])}, {}, {}
    p[1], p[3] = along_z(p[0], 1), along_z(p[0], 3)
    together(spectra_q, xp[0], p[1], p[3])
    p[2], xp[3] = along_z(p[3], 1), along_z(xp[0], 3)
    q[0] = Block(turn(spectra_q.value))
    together(q[0], p[2], xp[3])
    xq[0] = along_x(q[0])
    q[1], q[3] = along_z(q[0], 1), along_z(q[0], 3)
    p_other = to_core(*[p[k] for k in STEPS_Z])
    together(xq[0], q[1], q[3])
    xq[1] = along_x(q[1])
    xp[2], q[2] = along_z(xp[3], 1), along_z(q[1], 3)
    far_a = to_core(xp[0], xp[3], xq[0])
    together(xq[1], xp[2], q[2])
    xq[3] = along_x(q[3])
    xp[1], xq[2] = along_z(xp[0], 1), along_z(xq[1], 3)
    q_other = to_core(*[q[k] for k in STEPS_Z])
    far_b = to_core(xp[2], xq[1])
    token = Block(jnp.zeros((8, 128), jnp.float32))
    parts = [p[0].value, q[0].value]
    for at, k in enumerate(STEPS_Z):
        parts += [p[k].value, (p_other, at), q[k].value, (q_other, at)]
    out, token.value = correlate(0, place, scale, parts, token.value)
    together(token, xq[3], xp[1], xq[2])
    far_c = to_core(xp[1], xq[3], xq[2])
    parts = [p[0].value, q[0].value]
    parts += [xp[0].value, (far_a, 0), xq[0].value, (far_a, 2)]
    parts += [xp[1].value, (far_c, 0), xq[1].value, (far_b, 1)]
    parts += [xp[3].value, (far_a, 1), xq[3].value, (far_c, 1)]
    parts += [xp[2].value, (far_b, 0), xq[2].value, (far_c, 2)]
    return correlate(1, place, scale, parts, token.value, out)[0]


def solution(mesh):
    names = ("y", "x_lo", "x_hi", "z", "core")
    mesh = jax.sharding.Mesh(mesh.devices.reshape(4, 2, 2, 4, 2), names)
    in_specs = (P(None, ("x_hi", "z", "core"), ("y", "x_lo"), None), P(), P(), P())
    out_specs = P(("y", "x_lo"), None, ("x_hi", "z", "core"), None)
    return jax.shard_map(
        on_device, mesh=mesh, in_specs=in_specs, out_specs=out_specs, check_vma=False
    )
```

```python
import functools
import math

import jax
import jax.numpy as jnp
import ml_dtypes
import numpy as np
from jax import lax
from jax.experimental import pallas as pl
from jax.experimental.pallas import tpu as pltpu
from jax.sharding import PartitionSpec as P

NFFT = 4096
HALF = NFFT // 2
TAPS = 4
FRAMES = 128
CHUNK = 64


def dft_tables():
    n = np.arange(HALF)[:, None]
    tables = []
    for cls in range(2):
        channel = 2 * np.arange(128)[None, :] + cls
        angle = 2.0 * np.pi * ((n * channel) % NFFT) / NFFT
        table = np.concatenate([np.cos(angle), np.sin(angle)], axis=1)
        high = table.astype(ml_dtypes.bfloat16)
        low = (table - high.astype(np.float64)).astype(ml_dtypes.bfloat16)
        tables.append(np.stack([high, low]))
    return np.stack(tables)


BLOCK = 256
BLOCKS = HALF // BLOCK


def spectra_kernel(
    first_frame, count, last, x_hbm, taps_ref, table_hbm, flags_ref, before_ref, out_ref,
    x_vmem, table, fold_a, fold_b, total, sums, turned, x_sems, table_sems,
):
    frames = count + TAPS - 1
    rows = count * 8
    x_copies, table_copies = [], []
    for kb in range(BLOCKS):
        for half in range(2):
            lanes = pl.ds(half * HALF + kb * BLOCK, BLOCK)
            x_copies.append(
                pltpu.make_async_copy(
                    x_hbm.at[:, pl.ds(first_frame, frames), :, lanes],
                    x_vmem.at[:, :, :, lanes],
                    x_sems.at[kb, half],
                )
            )
        samples = pl.ds(kb * BLOCK, BLOCK)
        table_copies.append(
            pltpu.make_async_copy(table_hbm.at[:, :, samples], table.at[:, :, samples], table_sems.at[kb])
        )

    def fetch(kb):
        x_copies[2 * kb].start()
        x_copies[2 * kb + 1].start()
        table_copies[kb].start()

    fetch(0)
    fetch(1)

    def fir(kb, p, tile, fold):
        n0 = pl.multiple_of(kb * BLOCK + tile * 128, 128)
        to = pl.ds(pl.multiple_of(tile * 128, 128), 128)

        def load(f, offset):
            return x_vmem[p, f, :, pl.ds(n0 + offset, 128)].astype(jnp.float32)

        def tap(k, offset):
            return jnp.broadcast_to(taps_ref[k : k + 1, pl.ds(n0 + offset, 128)], (8, 128))

        taps = [[tap(k, offset) for k in range(TAPS)] for offset in (0, HALF)]
        window = [[load(f, offset) for f in range(TAPS - 1)] for offset in (0, HALF)]
        for pair in range(count // 2):
            even, odd = [], []
            for f in (2 * pair, 2 * pair + 1):
                halves = []
                for w, h, offset in zip(window, taps, (0, HALF)):
                    w.append(load(f + TAPS - 1, offset))
                    halves.append(((w[0] * h[0] + w[1] * h[1]) + w[2] * h[2]) + w[3] * h[3])
                    w.pop(0)
                even.append(halves[0] + halves[1])
                odd.append(halves[0] - halves[1])
            for cls, both in enumerate((even, odd)):
                value = jnp.concatenate(both, axis=0)
                high = value.astype(jnp.bfloat16)
                low = (value - high.astype(jnp.float32)).astype(jnp.bfloat16)
                fold[p, cls, 0, pair * 16 : pair * 16 + 16, to] = high
                fold[p, cls, 1, pair * 16 : pair * 16 + 16, to] = low

    def product(kb, cls, p, fold):
        samples = pl.ds(pl.multiple_of(kb * BLOCK, BLOCK), BLOCK)
        high, low = fold[p, cls, 0], fold[p, cls, 1]
        left = jnp.concatenate([high, low, high], axis=1)
        table_high, table_low = table[cls, 0, samples, :], table[cls, 1, samples, :]
        right = jnp.concatenate([table_high, table_high, table_low], axis=0)
        return jnp.dot(left, right, preferred_element_type=jnp.float32)

    def stage(kb, fold_in, fold_out, first=False):
        def unit(a, carry):
            if fold_out is not None:
                fir(kb + 1, a, 0, fold_out)
                fir(kb + 1, a, 1, fold_out)
            for b in range(2):
                if fold_in is not None:
                    value = product(kb, a, b, fold_in)
                    if first:
                        total[a, b] = value
                    else:
                        total[a, b] += value
            return carry

        lax.fori_loop(0, 2, unit, 0)

    def arrive(kb):
        x_copies[2 * kb].wait()
        x_copies[2 * kb + 1].wait()
        table_copies[kb].wait()

    arrive(0)
    for kb in range(2, BLOCKS):
        fetch(kb)
    stage(-1, None, fold_a)
    arrive(1)
    stage(0, fold_a, fold_b, first=True)
    arrive(2)
    stage(1, fold_b, fold_a)
    for kb in range(3, BLOCKS):
        arrive(kb)

    def two_stages(k, carry):
        stage(2 * k, fold_a, fold_b)
        stage(2 * k + 1, fold_b, fold_a)
        return carry

    lax.fori_loop(1, BLOCKS // 2 - 1, two_stages, 0)
    stage(BLOCKS - 2, fold_a, fold_b)
    stage(BLOCKS - 1, fold_b, None)
    blk = (lax.axis_index("x_hi") * 4 + lax.axis_index("z")) * 2 + lax.axis_index("core")
    chan = lax.axis_index("y") * 2 + lax.axis_index("x_lo")
    station = lax.broadcasted_iota(jnp.int32, (8, 128), 0) // 2
    weight = jnp.zeros((8, 128), jnp.float32)
    for k in range(4):
        flag = flags_ref[blk * 32 + chan * 4 + k].astype(jnp.float32) / math.sqrt(2.0 * NFFT)
        weight = jnp.where(station == k, flag, weight)
    for cls in range(2):
        real = total[cls, 0, :, :128] + total[cls, 1, :, 128:]
        imag = total[cls, 1, :, :128] - total[cls, 0, :, 128:]
        for plane, value in enumerate((real, imag)):
            value = (value.reshape(count, 8, 128) * weight).reshape(rows, 128)
            if not last:
                out_ref[cls, plane] = value
                continue
            end = (plane + 1) * CHUNK * 8
            sums[cls, end - rows : end, :] = value
            if count < CHUNK:
                sums[cls, end - CHUNK * 8 : end - rows, :] = before_ref[cls, plane]
    if not last:
        return
    for cls in range(2):
        for i in range(8):
            turned[cls, i * 128 : (i + 1) * 128, :] = sums[cls, pl.ds(i, 128, stride=8), :].T

    def emit(g, carry):
        for cls in range(2):
            for j in range(16):
                out_ref[g, cls, j] = turned[cls, pl.ds(g * 16 + j, 8, stride=128), :].astype(jnp.bfloat16)
        return carry

    lax.fori_loop(0, 8, emit, 0)


def spectra(first_frame, count, last, x, taps, tables, flags, before):
    if last:
        out_shape = jax.ShapeDtypeStruct((8, 2, 16, 8, 128), jnp.bfloat16)
    else:
        out_shape = jax.ShapeDtypeStruct((2, 2, count * 8, 128), jnp.float32)
    return pl.pallas_call(
        functools.partial(spectra_kernel, first_frame, count, last),
        out_shape=out_shape,
        in_specs=[
            pl.BlockSpec(memory_space=pltpu.HBM),
            pl.BlockSpec(memory_space=pltpu.VMEM),
            pl.BlockSpec(memory_space=pltpu.HBM),
            pl.BlockSpec(memory_space=pltpu.SMEM),
            pl.BlockSpec(memory_space=pltpu.VMEM),
        ],
        out_specs=pl.BlockSpec(memory_space=pltpu.VMEM),
        scratch_shapes=[
            pltpu.VMEM((2, count + TAPS - 1, 8, NFFT), jnp.bfloat16),
            pltpu.VMEM((2, 2, HALF, 256), jnp.bfloat16),
            pltpu.VMEM((2, 2, 2, count * 8, BLOCK), jnp.bfloat16),
            pltpu.VMEM((2, 2, 2, count * 8, BLOCK), jnp.bfloat16),
            pltpu.VMEM((2, 2, count * 8, 256), jnp.float32),
            pltpu.VMEM((2, 2 * CHUNK * 8, 128), jnp.float32),
            pltpu.VMEM((2, 8 * 128, 128), jnp.float32),
            pltpu.SemaphoreType.DMA((BLOCKS, 2)),
            pltpu.SemaphoreType.DMA((BLOCKS,)),
        ],
        compiler_params=pltpu.CompilerParams(vmem_limit_bytes=56 * 1024 * 1024),
        cost_estimate=pl.CostEstimate(
            flops=100_000_000 * count, bytes_accessed=140_000 * count + 4_000_000, transcendentals=0
        ),
        name="spectra",
    )(x, taps, tables, flags, before)


NJ = 4


STEPS_Z = (0, 1, 3, 2)


def correlate_kernel(pairs, places, place_ref, scale_ref, *refs):
    out_ref, token_ref, staged, sems = refs[-4:]
    step, steps = pl.program_id(0), pl.num_programs(0)
    slot = step % 2
    at_core_0 = place_ref[2] == 0
    token_ref[...] = jnp.zeros_like(token_ref)

    def copies(at):
        made = []
        for q, (far, bits) in enumerate(pairs):
            column = pl.multiple_of((place_ref[0] ^ far) * 512 + (place_ref[1] ^ bits) * 128, 128)
            made.append(
                pltpu.make_async_copy(
                    staged.at[at % 2, q],
                    out_ref.at[pl.ds(at * (2 * NJ), 2 * NJ), :, :, pl.ds(column, 128)],
                    sems.at[at % 2, q],
                )
            )
        return made

    @pl.when(step >= 2)
    def _():
        for copy in copies(step - 2):
            copy.wait()

    lane = lax.broadcasted_iota(jnp.int32, (64, 128), 1)
    sign = jnp.where(lane < 64, 1.0, -1.0)
    for cls in range(2):
        for jj in range(NJ):

            def load(place):
                ref, *lead = place
                return refs[ref][(*lead, cls, jj)]

            own = [load(place) for place in places[:2]]
            turned = [(pltpu.roll(o.astype(jnp.float32), 64, 1) * sign).astype(jnp.bfloat16) for o in own]
            left = jnp.concatenate([jnp.concatenate(own, axis=1), jnp.concatenate(turned, axis=1)], axis=0)
            channel = 2 * jj + cls
            scale = scale_ref[step * (2 * NJ) + channel]
            for q in range(0, len(pairs), 2):
                group = range(q, min(q + 2, len(pairs)))
                rows = []
                for k in group:
                    same_p, other_p, same_q, other_q = [load(place) for place in places[2 + 4 * k : 6 + 4 * k]]
                    same = jnp.concatenate([same_p, same_q], axis=1)
                    other = jnp.concatenate([other_p, other_q], axis=1)
                    rows += [jnp.where(at_core_0, same, other), jnp.where(at_core_0, other, same)]
                right = jnp.concatenate(rows, axis=0)
                total = lax.dot_general(
                    left, right, (((1,), (1,)), ((), ())), preferred_element_type=jnp.float32
                )
                total = (total * scale).astype(jnp.bfloat16)
                for k in group:
                    lanes = slice(128 * (k - q), 128 * (k - q) + 128)
                    for plane in range(2):
                        staged[slot, k, channel, plane] = total[64 * plane : 64 * plane + 64, lanes]
    for copy in copies(step):
        copy.start()

    @pl.when(step == steps - 1)
    def _():
        for at in (steps - 2, steps - 1):
            for copy in copies(at):
                copy.wait()


def block_index(lead, step):
    return (0,) * lead + (step, 0, 0)


def correlate(pairs, place, scale, parts, token, out=None):
    operands, places = [], []
    for part in parts:
        array, *lead = part if isinstance(part, tuple) else (part,)
        known = [at for at, operand in enumerate(operands) if operand is array]
        if not known:
            operands.append(array)
        places.append((known[0] if known else len(operands) - 1, *lead))
    specs = [pl.BlockSpec(memory_space=pltpu.SMEM)] * 2
    for block in operands:
        lead = block.shape[:-4]
        specs.append(pl.BlockSpec((*lead, 2, NJ, 64, 128), functools.partial(block_index, len(lead) + 1)))
    specs.append(pl.BlockSpec(memory_space=pltpu.HBM))
    operands.append(token)
    aliases = {}
    if out is not None:
        specs.append(pl.BlockSpec(memory_space=pltpu.HBM))
        aliases = {2 + len(operands): 0}
        operands.append(out)
    return pl.pallas_call(
        functools.partial(correlate_kernel, pairs, places),
        out_shape=(
            jax.ShapeDtypeStruct((32, 2, 64, 1024), jnp.bfloat16),
            jax.ShapeDtypeStruct((8, 128), jnp.float32),
        ),
        grid=(16 // NJ,),
        in_specs=specs,
        out_specs=(pl.BlockSpec(memory_space=pltpu.HBM), pl.BlockSpec((8, 128), lambda s: (0, 0))),
        input_output_aliases=aliases,
        scratch_shapes=[
            pltpu.VMEM((2, len(pairs), 2 * NJ, 2, 64, 128), jnp.bfloat16),
            pltpu.SemaphoreType.DMA((2, len(pairs))),
        ],
        compiler_params=pltpu.CompilerParams(vmem_limit_bytes=56 * 1024 * 1024),
        cost_estimate=pl.CostEstimate(flops=500_000_000 * len(pairs), bytes_accessed=3_300_000 * len(pairs), transcendentals=0),
        name="correlate",
    )(place, scale, *operands)


class Block:
    def __init__(self, value):
        self.value = value


def together(*blocks):
    values = lax.optimization_barrier(tuple(block.value for block in blocks))
    for block, value in zip(blocks, values):
        block.value = value


def along_x(block):
    return Block(lax.ppermute(block.value, "x_hi", [(0, 1), (1, 0)]))


def along_z(block, bits):
    return Block(lax.ppermute(block.value, "z", [(z, z ^ bits) for z in range(4)]))


def to_core(*blocks):
    array = blocks[0].value if len(blocks) == 1 else jnp.stack([block.value for block in blocks])
    return lax.ppermute(array, "core", [(0, 1), (1, 0)])


def turn(chunk):
    got = lax.all_to_all(chunk, ("y", "x_lo"), split_axis=0, concat_axis=0, tiled=True)
    return got.transpose(1, 2, 0, 3, 4).reshape(2, 16, 64, 128)


def on_device(voltages, fir_taps, station_flags, bin_offsets):
    chan = lax.axis_index(("y", "x_lo"))
    x_hi, z, core = [lax.axis_index(axis) for axis in ("x_hi", "z", "core")]
    scales = jnp.exp2(-bin_offsets.astype(jnp.float32)) / FRAMES
    scale = lax.dynamic_slice_in_dim(scales, chan * 32, 32, 0)
    tables = jnp.asarray(dft_tables())
    planes = voltages.reshape(2, 8, FRAMES + TAPS - 1, NFFT).transpose(0, 2, 1, 3)

    place = jnp.stack([x_hi, z, core]).astype(jnp.int32)
    p = {0: Block(turn(spectra(0, CHUNK, True, planes, fir_taps, tables, station_flags, fir_taps)))}
    part = Block(spectra(CHUNK, CHUNK // 2, False, planes, fir_taps, tables, station_flags, fir_taps))
    together(part, p[0])
    spectra_q = Block(
        spectra(CHUNK + CHUNK // 2, CHUNK // 2, True, planes, fir_taps, tables, station_flags, part.value)
    )
    xp, q, xq = {0: along_x(p[0])}, {}, {}
    p[1], p[3] = along_z(p[0], 1), along_z(p[0], 3)
    together(spectra_q, xp[0], p[1], p[3])
    p[2], xp[3] = along_z(p[3], 1), along_z(xp[0], 3)
    q[0] = Block(turn(spectra_q.value))
    xq[0] = along_x(q[0])
    from_0 = Block(q[0].value), Block(q[0].value)
    together(from_0[0], p[2])
    together(from_0[1], xp[3])
    q[1], q[3] = along_z(from_0[0], 1), along_z(from_0[1], 3)
    together(q[1], xq[0])
    xq[1] = along_x(q[1])
    others_a = to_core(*[p[k] for k in STEPS_Z], xp[0], xp[3], xq[0])
    from_3 = Block(xp[3].value)
    together(from_3, q[1])
    xp[2] = along_z(from_3, 1)
    together(q[3], q[1])
    q[2] = along_z(q[1], 3)
    together(q[3], xq[1])
    xq[3] = along_x(q[3])
    from_0 = Block(xp[0].value)
    together(from_0, xp[2])
    xp[1] = along_z(from_0, 1)
    together(xq[1], q[2])
    xq[2] = along_z(xq[1], 3)
    others_b = to_core(*[q[k] for k in STEPS_Z], xp[2], xq[1])
    token = Block(jnp.zeros((8, 128), jnp.float32))
    own = [p[0].value, q[0].value]
    parts = list(own)
    for at, k in enumerate(STEPS_Z):
        parts += [p[k].value, (others_a, at), q[k].value, (others_b, at)]
    parts += [xp[0].value, (others_a, 4), xq[0].value, (others_a, 6)]
    early = [(0, k) for k in STEPS_Z] + [(1, 0)]
    out, token.value = correlate(early, place, scale, parts, token.value)
    together(token, xq[3], xp[1], xq[2])
    parts = list(own)
    parts += [xp[1].value, to_core(xp[1]), xq[1].value, (others_b, 5)]
    parts += [xp[3].value, (others_a, 5), xq[3].value, to_core(xq[3])]
    parts += [xp[2].value, (others_b, 4), xq[2].value, to_core(xq[2])]
    return correlate([(1, 1), (1, 3), (1, 2)], place, scale, parts, token.value, out)[0]


def solution(mesh):
    names = ("y", "x_lo", "x_hi", "z", "core")
    mesh = jax.sharding.Mesh(mesh.devices.reshape(4, 2, 2, 4, 2), names)
    in_specs = (P(None, ("x_hi", "z", "core"), ("y", "x_lo"), None), P(), P(), P())
    out_specs = P(("y", "x_lo"), None, ("x_hi", "z", "core"), None)
    return jax.shard_map(
        on_device, mesh=mesh, in_specs=in_specs, out_specs=out_specs, check_vma=False
    )
```

```python
import functools
import math

import jax
import jax.numpy as jnp
import ml_dtypes
import numpy as np
from jax import lax
from jax.experimental import pallas as pl
from jax.experimental.pallas import tpu as pltpu
from jax.sharding import PartitionSpec as P

NFFT = 4096
HALF = NFFT // 2
TAPS = 4
FRAMES = 128
CHUNK = 64


def dft_tables():
    n = np.arange(HALF)[:, None]
    tables = []
    for cls in range(2):
        channel = 2 * np.arange(128)[None, :] + cls
        angle = 2.0 * np.pi * ((n * channel) % NFFT) / NFFT
        table = np.concatenate([np.cos(angle), np.sin(angle)], axis=1)
        high = table.astype(ml_dtypes.bfloat16)
        low = (table - high.astype(np.float64)).astype(ml_dtypes.bfloat16)
        tables.append(np.stack([high, low]))
    return np.stack(tables)


BLOCK = 256
BLOCKS = HALF // BLOCK


def spectra_kernel(
    first_frame, count, last, x_hbm, taps_ref, table_hbm, flags_ref, before_ref, out_ref,
    x_vmem, table, fold_a, fold_b, total, sums, turned, x_sems, table_sems,
):
    frames = count + TAPS - 1
    rows = count * 8
    x_copies, table_copies = [], []
    for kb in range(BLOCKS):
        for half in range(2):
            lanes = pl.ds(half * HALF + kb * BLOCK, BLOCK)
            x_copies.append(
                pltpu.make_async_copy(
                    x_hbm.at[:, pl.ds(first_frame, frames), :, lanes],
                    x_vmem.at[:, :, :, lanes],
                    x_sems.at[kb, half],
                )
            )
        samples = pl.ds(kb * BLOCK, BLOCK)
        table_copies.append(
            pltpu.make_async_copy(table_hbm.at[:, :, samples], table.at[:, :, samples], table_sems.at[kb])
        )

    def fetch(kb):
        x_copies[2 * kb].start()
        x_copies[2 * kb + 1].start()
        table_copies[kb].start()

    fetch(0)
    fetch(1)

    def fir(kb, p, tile, fold):
        n0 = pl.multiple_of(kb * BLOCK + tile * 128, 128)
        to = pl.ds(pl.multiple_of(tile * 128, 128), 128)

        def load(f, offset):
            return x_vmem[p, f, :, pl.ds(n0 + offset, 128)].astype(jnp.float32)

        def tap(k, offset):
            return jnp.broadcast_to(taps_ref[k : k + 1, pl.ds(n0 + offset, 128)], (8, 128))

        taps = [[tap(k, offset) for k in range(TAPS)] for offset in (0, HALF)]
        window = [[load(f, offset) for f in range(TAPS - 1)] for offset in (0, HALF)]
        for pair in range(count // 2):
            even, odd = [], []
            for f in (2 * pair, 2 * pair + 1):
                halves = []
                for w, h, offset in zip(window, taps, (0, HALF)):
                    w.append(load(f + TAPS - 1, offset))
                    halves.append(((w[0] * h[0] + w[1] * h[1]) + w[2] * h[2]) + w[3] * h[3])
                    w.pop(0)
                even.append(halves[0] + halves[1])
                odd.append(halves[0] - halves[1])
            for cls, both in enumerate((even, odd)):
                value = jnp.concatenate(both, axis=0)
                high = value.astype(jnp.bfloat16)
                low = (value - high.astype(jnp.float32)).astype(jnp.bfloat16)
                fold[p, cls, 0, pair * 16 : pair * 16 + 16, to] = high
                fold[p, cls, 1, pair * 16 : pair * 16 + 16, to] = low

    def product(kb, cls, p, fold):
        samples = pl.ds(pl.multiple_of(kb * BLOCK, BLOCK), BLOCK)
        planes = range(2) if p is None else (p,)
        left = [[fold[plane, cls, part] for part in (0, 1, 0)] for plane in planes]
        left = jnp.concatenate([jnp.concatenate(parts, axis=1) for parts in left], axis=0)
        table_high, table_low = table[cls, 0, samples, :], table[cls, 1, samples, :]
        right = jnp.concatenate([table_high, table_high, table_low], axis=0)
        return jnp.dot(left, right, preferred_element_type=jnp.float32)

    def stage(kb, fold_in, fold_out, first=False):
        def unit(a, carry):
            if fold_out is not None:
                fir(kb + 1, a, 0, fold_out)
                fir(kb + 1, a, 1, fold_out)
            both = product(kb, a, None, fold_in) if fold_in is not None and count < CHUNK else None
            for b in range(2):
                if fold_in is not None:
                    value = product(kb, a, b, fold_in) if both is None else both[b * rows : (b + 1) * rows]
                    if first:
                        total[a, b] = value
                    else:
                        total[a, b] += value
            return carry

        lax.fori_loop(0, 2, unit, 0)

    def arrive(kb):
        x_copies[2 * kb].wait()
        x_copies[2 * kb + 1].wait()
        table_copies[kb].wait()

    arrive(0)
    for kb in range(2, BLOCKS):
        fetch(kb)
    stage(-1, None, fold_a)
    arrive(1)
    stage(0, fold_a, fold_b, first=True)
    arrive(2)
    stage(1, fold_b, fold_a)
    for kb in range(3, BLOCKS):
        arrive(kb)

    def two_stages(k, carry):
        stage(2 * k, fold_a, fold_b)
        stage(2 * k + 1, fold_b, fold_a)
        return carry

    lax.fori_loop(1, BLOCKS // 2 - 1, two_stages, 0)
    stage(BLOCKS - 2, fold_a, fold_b)
    stage(BLOCKS - 1, fold_b, None)
    blk = (lax.axis_index("x_hi") * 4 + lax.axis_index("z")) * 2 + lax.axis_index("core")
    chan = lax.axis_index("y") * 2 + lax.axis_index("x_lo")
    station = lax.broadcasted_iota(jnp.int32, (8, 128), 0) // 2
    weight = jnp.zeros((8, 128), jnp.float32)
    for k in range(4):
        flag = flags_ref[blk * 32 + chan * 4 + k].astype(jnp.float32) / math.sqrt(2.0 * NFFT)
        weight = jnp.where(station == k, flag, weight)
    for cls in range(2):
        real = total[cls, 0, :, :128] + total[cls, 1, :, 128:]
        imag = total[cls, 1, :, :128] - total[cls, 0, :, 128:]
        for plane, value in enumerate((real, imag)):
            value = (value.reshape(count, 8, 128) * weight).reshape(rows, 128)
            if not last:
                out_ref[cls, plane] = value
                continue
            end = (plane + 1) * CHUNK * 8
            sums[cls, end - rows : end, :] = value
            if count < CHUNK:
                sums[cls, end - CHUNK * 8 : end - rows, :] = before_ref[cls, plane]
    if not last:
        return
    for cls in range(2):
        for i in range(8):
            turned[cls, i * 128 : (i + 1) * 128, :] = sums[cls, pl.ds(i, 128, stride=8), :].T

    def emit(g, carry):
        for cls in range(2):
            for j in range(16):
                out_ref[g, cls, j] = turned[cls, pl.ds(g * 16 + j, 8, stride=128), :].astype(jnp.bfloat16)
        return carry

    lax.fori_loop(0, 8, emit, 0)


def spectra(first_frame, count, last, x, taps, tables, flags, before):
    if last:
        out_shape = jax.ShapeDtypeStruct((8, 2, 16, 8, 128), jnp.bfloat16)
    else:
        out_shape = jax.ShapeDtypeStruct((2, 2, count * 8, 128), jnp.float32)
    return pl.pallas_call(
        functools.partial(spectra_kernel, first_frame, count, last),
        out_shape=out_shape,
        in_specs=[
            pl.BlockSpec(memory_space=pltpu.HBM),
            pl.BlockSpec(memory_space=pltpu.VMEM),
            pl.BlockSpec(memory_space=pltpu.HBM),
            pl.BlockSpec(memory_space=pltpu.SMEM),
            pl.BlockSpec(memory_space=pltpu.VMEM),
        ],
        out_specs=pl.BlockSpec(memory_space=pltpu.VMEM),
        scratch_shapes=[
            pltpu.VMEM((2, count + TAPS - 1, 8, NFFT), jnp.bfloat16),
            pltpu.VMEM((2, 2, HALF, 256), jnp.bfloat16),
            pltpu.VMEM((2, 2, 2, count * 8, BLOCK), jnp.bfloat16),
            pltpu.VMEM((2, 2, 2, count * 8, BLOCK), jnp.bfloat16),
            pltpu.VMEM((2, 2, count * 8, 256), jnp.float32),
            pltpu.VMEM((2, 2 * CHUNK * 8, 128), jnp.float32),
            pltpu.VMEM((2, 8 * 128, 128), jnp.float32),
            pltpu.SemaphoreType.DMA((BLOCKS, 2)),
            pltpu.SemaphoreType.DMA((BLOCKS,)),
        ],
        compiler_params=pltpu.CompilerParams(vmem_limit_bytes=56 * 1024 * 1024),
        cost_estimate=pl.CostEstimate(
            flops=100_000_000 * count, bytes_accessed=140_000 * count + 4_000_000, transcendentals=0
        ),
        name="spectra",
    )(x, taps, tables, flags, before)


NJ = 4


STEPS_Z = (0, 1, 3, 2)


def correlate_kernel(pairs, places, place_ref, scale_ref, *refs):
    out_ref, token_ref, staged, sems = refs[-4:]
    step, steps = pl.program_id(0), pl.num_programs(0)
    slot = step % 2
    at_core_0 = place_ref[2] == 0
    token_ref[...] = jnp.zeros_like(token_ref)

    def copies(at):
        made = []
        for q, (far, bits) in enumerate(pairs):
            column = pl.multiple_of((place_ref[0] ^ far) * 512 + (place_ref[1] ^ bits) * 128, 128)
            made.append(
                pltpu.make_async_copy(
                    staged.at[at % 2, q],
                    out_ref.at[pl.ds(at * (2 * NJ), 2 * NJ), :, :, pl.ds(column, 128)],
                    sems.at[at % 2, q],
                )
            )
        return made

    @pl.when(step >= 2)
    def _():
        for copy in copies(step - 2):
            copy.wait()

    lane = lax.broadcasted_iota(jnp.int32, (64, 128), 1)
    sign = jnp.where(lane < 64, 1.0, -1.0)
    for cls in range(2):
        for jj in range(NJ):

            def load(place):
                ref, *lead = place
                return refs[ref][(*lead, cls, jj)]

            own = [load(place) for place in places[:2]]
            turned = [(pltpu.roll(o.astype(jnp.float32), 64, 1) * sign).astype(jnp.bfloat16) for o in own]
            left = jnp.concatenate([jnp.concatenate(own, axis=1), jnp.concatenate(turned, axis=1)], axis=0)
            channel = 2 * jj + cls
            scale = scale_ref[step * (2 * NJ) + channel]
            for q in range(0, len(pairs), 2):
                group = range(q, min(q + 2, len(pairs)))
                rows = []
                for k in group:
                    same_p, other_p, same_q, other_q = [load(place) for place in places[2 + 4 * k : 6 + 4 * k]]
                    same = jnp.concatenate([same_p, same_q], axis=1)
                    other = jnp.concatenate([other_p, other_q], axis=1)
                    rows += [jnp.where(at_core_0, same, other), jnp.where(at_core_0, other, same)]
                right = jnp.concatenate(rows, axis=0)
                total = lax.dot_general(
                    left, right, (((1,), (1,)), ((), ())), preferred_element_type=jnp.float32
                )
                total = (total * scale).astype(jnp.bfloat16)
                for k in group:
                    lanes = slice(128 * (k - q), 128 * (k - q) + 128)
                    for plane in range(2):
                        staged[slot, k, channel, plane] = total[64 * plane : 64 * plane + 64, lanes]
    for copy in copies(step):
        copy.start()

    @pl.when(step == steps - 1)
    def _():
        for at in (steps - 2, steps - 1):
            for copy in copies(at):
                copy.wait()


def block_index(lead, step):
    return (0,) * lead + (step, 0, 0)


def correlate(pairs, place, scale, parts, token, out=None):
    operands, places = [], []
    for part in parts:
        array, *lead = part if isinstance(part, tuple) else (part,)
        known = [at for at, operand in enumerate(operands) if operand is array]
        if not known:
            operands.append(array)
        places.append((known[0] if known else len(operands) - 1, *lead))
    specs = [pl.BlockSpec(memory_space=pltpu.SMEM)] * 2
    for block in operands:
        lead = block.shape[:-4]
        specs.append(pl.BlockSpec((*lead, 2, NJ, 64, 128), functools.partial(block_index, len(lead) + 1)))
    specs.append(pl.BlockSpec(memory_space=pltpu.HBM))
    operands.append(token)
    aliases = {}
    if out is not None:
        specs.append(pl.BlockSpec(memory_space=pltpu.HBM))
        aliases = {2 + len(operands): 0}
        operands.append(out)
    return pl.pallas_call(
        functools.partial(correlate_kernel, pairs, places),
        out_shape=(
            jax.ShapeDtypeStruct((32, 2, 64, 1024), jnp.bfloat16),
            jax.ShapeDtypeStruct((8, 128), jnp.float32),
        ),
        grid=(16 // NJ,),
        in_specs=specs,
        out_specs=(pl.BlockSpec(memory_space=pltpu.HBM), pl.BlockSpec((8, 128), lambda s: (0, 0))),
        input_output_aliases=aliases,
        scratch_shapes=[
            pltpu.VMEM((2, len(pairs), 2 * NJ, 2, 64, 128), jnp.bfloat16),
            pltpu.SemaphoreType.DMA((2, len(pairs))),
        ],
        compiler_params=pltpu.CompilerParams(vmem_limit_bytes=56 * 1024 * 1024),
        cost_estimate=pl.CostEstimate(flops=500_000_000 * len(pairs), bytes_accessed=3_300_000 * len(pairs), transcendentals=0),
        name="correlate",
    )(place, scale, *operands)


class Block:
    def __init__(self, value):
        self.value = value


def together(*blocks):
    values = lax.optimization_barrier(tuple(block.value for block in blocks))
    for block, value in zip(blocks, values):
        block.value = value


def along_x(block):
    return Block(lax.ppermute(block.value, "x_hi", [(0, 1), (1, 0)]))


def along_z(block, bits):
    return Block(lax.ppermute(block.value, "z", [(z, z ^ bits) for z in range(4)]))


def to_core(*blocks):
    array = blocks[0].value if len(blocks) == 1 else jnp.stack([block.value for block in blocks])
    return lax.ppermute(array, "core", [(0, 1), (1, 0)])


def turn(chunk):
    got = lax.all_to_all(chunk, ("y", "x_lo"), split_axis=0, concat_axis=0, tiled=True)
    return got.transpose(1, 2, 0, 3, 4).reshape(2, 16, 64, 128)


def on_device(voltages, fir_taps, station_flags, bin_offsets):
    chan = lax.axis_index(("y", "x_lo"))
    x_hi, z, core = [lax.axis_index(axis) for axis in ("x_hi", "z", "core")]
    scales = jnp.exp2(-bin_offsets.astype(jnp.float32)) / FRAMES
    scale = lax.dynamic_slice_in_dim(scales, chan * 32, 32, 0)
    tables = jnp.asarray(dft_tables())
    planes = voltages.reshape(2, 8, FRAMES + TAPS - 1, NFFT).transpose(0, 2, 1, 3)

    place = jnp.stack([x_hi, z, core]).astype(jnp.int32)
    p = {0: Block(turn(spectra(0, CHUNK, True, planes, fir_taps, tables, station_flags, fir_taps)))}
    part = Block(spectra(CHUNK, CHUNK // 2, False, planes, fir_taps, tables, station_flags, fir_taps))
    together(part, p[0])
    spectra_q = Block(
        spectra(CHUNK + CHUNK // 2, CHUNK // 2, True, planes, fir_taps, tables, station_flags, part.value)
    )
    xp, q, xq = {0: along_x(p[0])}, {}, {}
    p[1], p[3] = along_z(p[0], 1), along_z(p[0], 3)
    together(spectra_q, xp[0], p[1], p[3])
    p[2], xp[3] = along_z(p[3], 1), along_z(xp[0], 3)
    q[0] = Block(turn(spectra_q.value))
    xq[0] = along_x(q[0])
    from_0 = Block(q[0].value), Block(q[0].value)
    together(from_0[0], p[2])
    together(from_0[1], xp[3])
    q[1], q[3] = along_z(from_0[0], 1), along_z(from_0[1], 3)
    together(q[1], xq[0])
    xq[1] = along_x(q[1])
    others_a = to_core(*[p[k] for k in STEPS_Z], xp[0], xp[3], xq[0])
    from_3 = Block(xp[3].value)
    together(from_3, q[1])
    xp[2] = along_z(from_3, 1)
    together(q[3], q[1])
    q[2] = along_z(q[1], 3)
    together(q[3], xq[1])
    xq[3] = along_x(q[3])
    from_0 = Block(xp[0].value)
    together(from_0, xp[2])
    xp[1] = along_z(from_0, 1)
    together(xq[1], q[2])
    xq[2] = along_z(xq[1], 3)
    others_b = to_core(*[q[k] for k in STEPS_Z], xp[2], xq[1])
    token = Block(jnp.zeros((8, 128), jnp.float32))
    own = [p[0].value, q[0].value]
    parts = list(own)
    for at, k in enumerate(STEPS_Z):
        parts += [p[k].value, (others_a, at), q[k].value, (others_b, at)]
    parts += [xp[0].value, (others_a, 4), xq[0].value, (others_a, 6)]
    early = [(0, k) for k in STEPS_Z] + [(1, 0)]
    out, token.value = correlate(early, place, scale, parts, token.value)
    together(token, xq[3], xp[1], xq[2])
    parts = list(own)
    parts += [xp[1].value, to_core(xp[1]), xq[1].value, (others_b, 5)]
    parts += [xp[3].value, (others_a, 5), xq[3].value, to_core(xq[3])]
    parts += [xp[2].value, (others_b, 4), xq[2].value, to_core(xq[2])]
    return correlate([(1, 1), (1, 3), (1, 2)], place, scale, parts, token.value, out)[0]


def solution(mesh):
    names = ("y", "x_lo", "x_hi", "z", "core")
    mesh = jax.sharding.Mesh(mesh.devices.reshape(4, 2, 2, 4, 2), names)
    in_specs = (P(None, ("x_hi", "z", "core"), ("y", "x_lo"), None), P(), P(), P())
    out_specs = P(("y", "x_lo"), None, ("x_hi", "z", "core"), None)
    return jax.shard_map(
        on_device, mesh=mesh, in_specs=in_specs, out_specs=out_specs, check_vma=False
    )
```
